512 devices in a mesh: aux: 64 (over y, z), fock: 8 (over x, core).
Axes of the slice: x: 4, y: 4, z: 16, core: 2. Of those that a mesh axis runs over, the one named last changes fastest.
Arguments:
- three_index: bfloat16 [512, 4096, 512], P('fock', 'aux'), may hold values from -0.25 to 0.25
- col_blocks: int32 [64, 8], replicated, may hold values from 0 to 63, as said below
- pair_mask: int32 [64, 8], replicated, may hold values 0 or 1
- occ_coef: bfloat16 [4096, 384], P('aux'), may hold values from -6 to 6
- occ_mask: int32 [64, 6], replicated, may hold values 0 or 1
- kept: int32 [128, 2], replicated, may hold values from 0 to 63, as said below
Outputs:
- exchange_blocks: float32 [128, 4096], P('fock', 'aux')
The draws below stay inside these ranges and needn't reach their ends.
Inputs may be any that keep to these rules, and one draw needn't show every extreme that they name: `col_blocks`: each row r names 8 different column blocks; the first is r itself, the second is either (r - 1) mod 64 or (r + 32) mod 64. `kept`: each pair names two different blocks and no ordered pair repeats; every row block is the first entry of exactly 2 pairs. The pairs stand in no particular order.
All inputs are finite; a program needn't handle non-finite values.
Results may differ from the reference program's by a relative error of at most 0.0039.
Values may be sent and summed in bfloat16 or wider, within the bound.
A program may use at most 64 MiB of HBM per device.

```python
import math
import jax
import jax.numpy as jnp
from jax import lax

BS = 64
NSIG = 8
NOCC = 384
NB = 64
NAO = 4096
NAUX = 512
NKEPT = 128


def distinct_offsets(key, count, first, skip_zero):
    candidates = jnp.arange(NB, dtype=jnp.int32)
    scores = jax.random.randint(key, (NB, NB), 0, 1 << 20) * NB + candidates[None, :]
    scores = jnp.where(candidates[None, :] == first, -1, scores)
    if skip_zero:
        scores = jnp.where(candidates[None, :] == 0, 1 << 30, scores)
    order = jnp.argsort(scores, axis=1, stable=True)
    return order[:, :count].astype(jnp.int32)


def draw_col_blocks(key, part):
    key = jax.random.fold_in(key, 11)
    candidates = jnp.arange(NB, dtype=jnp.int32)
    reserved = (candidates == 0) | (candidates == NB - 1) | (candidates == NB // 2)
    scores = jax.random.randint(jax.random.fold_in(key, 1), (NB, NB), 0, 1 << 20) * NB + candidates[None, :]
    scores = jnp.where(reserved[None, :], 1 << 30, scores)
    order = jnp.argsort(scores, axis=1, stable=True).astype(jnp.int32)
    rest = order[:, :NSIG - 2]
    flips = jax.random.randint(jax.random.fold_in(key, 2), (NB,), 0, 2).astype(jnp.int32)
    row_ids = jnp.arange(NB, dtype=jnp.int32)
    flips = jnp.where(row_ids == 0, 0, flips)
    flips = jnp.where(row_ids == 1, 1, flips)
    second = jnp.where(flips == 0, NB - 1, NB // 2).astype(jnp.int32)
    offsets = jnp.concatenate([jnp.zeros((NB, 1), jnp.int32), second[:, None], rest], axis=1)
    return ((row_ids[:, None] + offsets) % NB).astype(jnp.int32)


def draw_kept(key, part):
    key = jax.random.fold_in(key, 23)
    repeats = NKEPT // NB
    offsets = distinct_offsets(jax.random.fold_in(key, 1), repeats, -1, True)
    row_ids = jnp.arange(NB, dtype=jnp.int32)[:, None]
    columns = (row_ids + offsets) % NB
    row_part = jnp.broadcast_to(row_ids, (NB, repeats)).T.reshape(NKEPT)
    col_part = columns.T.reshape(NKEPT)
    pairs = jnp.stack([row_part, col_part], axis=1).astype(jnp.int32)
    shuffle = jax.random.permutation(jax.random.fold_in(key, 2), NKEPT)
    return pairs[shuffle].astype(jnp.int32)


def plant(drawn, own_key, low, largest):
    longest = drawn.shape.index(max(drawn.shape))
    spots = []
    for shift in (0, 1):
        where = [jax.random.randint(jax.random.fold_in(own_key, axis), (), 0, length) for axis, length in enumerate(drawn.shape)]
        where[longest] = (where[longest] + shift) % drawn.shape[longest]
        spots.append(tuple(where))
    return drawn.at[spots[0]].set(low).at[spots[1]].set(largest)


def levels(own_key, shape, split, smallest, top_value):
    factor_of = 1.0
    for position, parts in split:
        steps = jax.random.uniform(jax.random.fold_in(jax.random.fold_in(own_key, 6), position), (parts,), jnp.float32, smallest / len(split), top_value / len(split))
        factor_of = factor_of * jnp.repeat(jnp.exp(steps), shape[position] // parts).reshape((-1,) + (1,) * (len(shape) - 1 - position))
    return factor_of


def gaussian(rng, dims, scale, reach, cuts=(), kind=jnp.bfloat16):
    drawn = jax.random.normal(rng, dims, jnp.float32) * scale
    if len(cuts) > 0:
        drawn = levels(rng, dims, cuts, -0.22, 0.18) * drawn
    return jnp.clip(drawn, min=-reach, max=reach).astype(kind)


def setup_inputs(seed: int = 0) -> dict:
    splits = jax.random.split(jax.random.key(seed), 7)
    three_index = gaussian(splits[0], (NAUX, NAO, NSIG * BS), (NSIG * BS) ** -0.5, 0.25, ((0, 8), (1, 64)))
    col_blocks = draw_col_blocks(jax.random.fold_in(splits[6], 71), 0)
    pair_mask = plant((jax.random.randint(splits[2], (NB, NSIG), 0, 3) < 2).astype(jnp.int32), jax.random.fold_in(splits[2], 1), 0, 1)
    occ_coef = gaussian(splits[3], (NAO, NOCC), 1.0, 6.0, ((0, 64),))
    occ_mask = plant((jax.random.randint(splits[4], (NB, NOCC // BS), 0, 5) < 3).astype(jnp.int32), jax.random.fold_in(splits[4], 1), 0, 1)
    kept = draw_kept(jax.random.fold_in(splits[6], 71), 0)
    return dict(three_index=three_index, col_blocks=col_blocks, pair_mask=pair_mask, occ_coef=occ_coef, occ_mask=occ_mask, kept=kept)


def reference(three_index, col_blocks, pair_mask, occ_coef, occ_mask, kept):
    spread_mask = jnp.repeat(jnp.repeat(occ_mask, BS, axis=0), BS, axis=1)
    coef_masked = occ_coef * spread_mask.astype(jnp.bfloat16)
    coef_tiles = coef_masked.reshape(NB, BS, NOCC)
    picked = coef_tiles[col_blocks] * pair_mask.astype(jnp.bfloat16)[:, :, None, None]
    picked = picked.reshape(NB, NSIG * BS, NOCC).astype(jnp.float32)
    group = math.gcd(NAUX, 8)
    aux_slabs = three_index.reshape(NAUX // group, group, NB, BS, NSIG * BS)
    factor = float(NAUX * NOCC) ** -0.5

    def add_slab(accumulated, block_slab):
        half_block = jnp.einsum("pbmk,bki->pbmi", block_slab.astype(jnp.float32), picked)
        half_block = half_block.astype(jnp.bfloat16).astype(jnp.float32)
        left_rows = half_block[:, kept[:, 0]]
        right_rows = half_block[:, kept[:, 1]]
        return accumulated + jnp.einsum("pkmi,pkni->kmn", left_rows, right_rows), None

    start = jnp.zeros((NKEPT, BS, BS), jnp.float32)
    accumulated, _ = lax.scan(add_slab, start, aux_slabs)
    return (accumulated * factor).reshape(NKEPT, BS * BS)
```

```python
import jax
import jax.numpy as jnp
from jax import lax
from jax.experimental import pallas as pl
from jax.experimental.pallas import tpu as pltpu
from jax.sharding import PartitionSpec as P

MESH = pl.DeviceIdType.MESH
NY, NZ, NX, NC = 4, 16, 4, 2
NAUX_DEV = NY * NZ
BS = 64
SLOTS = 8
CHUNK = 128
CHUNKS = 3


def wait_for(ref, sem):
    pltpu.make_async_copy(ref, ref, sem).wait()


def kernel(factor, three_ref, colb_ref, pmask_ref, coef_ref, omask_ref, kept_ref, out_ref,
           tri, masked, g0, g1, x0, x1, w0, w1, w2, s0, s1, s2, r0, r1, r2, kacc, cb, xs, xb, ys, yb,
           vb, zs, zb, tsem, gsend, grecv, asend, arecv, csend, crecv, tsend, trecv):
    me = lax.axis_index("aux")
    fk = lax.axis_index("fock")
    y, z = me // NZ, me % NZ
    x, c = fk // NC, fk % NC
    sib = x * NC + (1 - c)

    load = pltpu.make_async_copy(three_ref, tri, tsem)
    load.start()

    bar = pltpu.get_barrier_semaphore()

    def greet(d, carry):
        pl.semaphore_signal(bar, inc=1, device_id=((me + d) % NAUX_DEV, fk), device_id_type=MESH)
        return carry

    lax.fori_loop(1, NAUX_DEV, greet, 0)
    for dx in range(1, NX):
        pl.semaphore_signal(bar, inc=1, device_id=(me, ((x + dx) % NX) * NC + c), device_id_type=MESH)
    pl.semaphore_signal(bar, inc=1, device_id=(me, sib), device_id_type=MESH)

    lane = lax.broadcasted_iota(jnp.int32, (BS, CHUNK), 1)
    for j in range(CHUNKS):
        m_lo = omask_ref[me, 2 * j].astype(jnp.float32)
        m_hi = omask_ref[me, 2 * j + 1].astype(jnp.float32)
        keep = jnp.where(lane < BS, m_lo, m_hi)
        part = coef_ref[:, j * CHUNK:(j + 1) * CHUNK].astype(jnp.float32) * keep
        masked[j] = part.astype(jnp.bfloat16).reshape(NX, 16, CHUNK)

    pl.semaphore_wait(bar, NAUX_DEV - 1 + NX - 1 + 1)

    def z_stage(w, g, chunk):
        def send(d, carry):
            tz = (z + d) % NZ
            pltpu.make_async_remote_copy(
                src_ref=masked.at[chunk, x], dst_ref=g.at[me],
                send_sem=gsend.at[3 * w], recv_sem=grecv.at[3 * w],
                device_id=(y * NZ + tz, fk), device_id_type=MESH).start()
            return carry
        lax.fori_loop(1, NZ, send, 0)
        g[me] = masked[chunk, x]

    def y_stage(w, g):
        wait_for(g.at[pl.ds(0, NZ - 1)], grecv.at[3 * w])
        for dy in range(1, NY):
            ty = (y + dy) % NY
            rows = g.at[pl.ds(y * NZ, NZ)]
            pltpu.make_async_remote_copy(
                src_ref=rows, dst_ref=rows,
                send_sem=gsend.at[3 * w + 1], recv_sem=grecv.at[3 * w + 1],
                device_id=(ty * NZ + z, fk), device_id_type=MESH).start()

    def x_stage(w, g, xsel, wt):
        wait_for(g.at[pl.ds(0, (NY - 1) * NZ)], grecv.at[3 * w + 1])
        for s in range(SLOTS):
            flag = pmask_ref[me, s].astype(jnp.float32)
            piece = g[colb_ref[me, s]].astype(jnp.float32) * flag
            piece = piece.astype(jnp.bfloat16)
            xsel[s] = piece
            wt[s, x] = piece
        for dx in range(1, NX):
            tx = (x + dx) % NX
            pltpu.make_async_remote_copy(
                src_ref=xsel, dst_ref=wt.at[:, x],
                send_sem=gsend.at[3 * w + 2], recv_sem=grecv.at[3 * w + 2],
                device_id=(me, tx * NC + c), device_id_type=MESH).start()

    def x_wait(w, wt):
        wait_for(wt.at[:, pl.ds(0, NX - 1)], grecv.at[3 * w + 2])

    def chunk_out(o, wt, s_ref, r_ref):
        def product(tz):
            rows = tri[:, tz].reshape(NY * BS, SLOTS * BS)
            weights = wt[...].reshape(SLOTS * BS, CHUNK)
            half = jnp.dot(rows, weights, preferred_element_type=jnp.float32)
            s_ref[:, tz] = half.astype(jnp.bfloat16).reshape(NY, BS, CHUNK)

        def send(ty, tz):
            pltpu.make_async_remote_copy(
                src_ref=s_ref.at[ty, tz], dst_ref=r_ref.at[me],
                send_sem=asend.at[o], recv_sem=arecv.at[o],
                device_id=(ty * NZ + tz, fk), device_id_type=MESH).start()

        def step(q, carry):
            dz = ((q + 1) // 2) * (2 * (q % 2) - 1)
            tz = (z + dz + NZ) % NZ
            product(tz)
            for dy in range(NY):
                send((y + dy) % NY, tz)
            return carry

        lax.fori_loop(1, NZ, step, 0)
        product(z)
        for dy in range(1, NY):
            send((y + dy) % NY, z)
        r_ref[me] = s_ref[y, z]

    pair_lane = lax.broadcasted_iota(jnp.int32, (BS, 2 * BS), 1)

    def group(o, r_ref, tx, tc):
        base = (tx * NC + tc) * 16
        for j in range(8):
            lo, hi = base + j, base + 8 + j
            left = jnp.concatenate([r_ref[kept_ref[lo, 0]], r_ref[kept_ref[hi, 0]]], axis=0)
            right = jnp.concatenate([r_ref[kept_ref[lo, 1]], r_ref[kept_ref[hi, 1]]], axis=0)
            both = lax.dot_general(left, right, (((1,), (1,)), ((), ())), preferred_element_type=jnp.float32)
            pick = jnp.where(pair_lane < BS, both[:BS], both[BS:]).reshape(NY, 16, 2 * BS)
            if o == 0:
                kacc[tx, tc, j] = pick
            else:
                kacc[tx, tc, j] += pick

    z_stage(0, g0, c)
    z_stage(1, g1, 2)
    y_stage(0, g0)
    y_stage(1, g1)
    x_stage(0, g0, x0, w0)
    load.wait()
    x_wait(0, w0)
    swap = pltpu.make_async_remote_copy(
        src_ref=w0, dst_ref=w1, send_sem=gsend.at[6], recv_sem=grecv.at[6],
        device_id=(me, sib), device_id_type=MESH)
    swap.start()
    chunk_out(0, w0, s0, r0)
    x_stage(1, g1, x1, w2)
    swap.wait()
    chunk_out(1, w1, s1, r1)
    x_wait(1, w2)
    chunk_out(2, w2, s2, r2)

    for o, r_ref in ((0, r0), (1, r1)):
        wait_for(r_ref.at[pl.ds(0, NAUX_DEV - 1)], arecv.at[o])

        def all_groups(t, carry):
            group(o, r_ref, t // NC, t % NC)
            return carry

        lax.fori_loop(0, NX * NC, all_groups, 0)

    wait_for(r2.at[pl.ds(0, NAUX_DEV - 1)], arecv.at[2])

    def core_copy(tx):
        return pltpu.make_async_remote_copy(
            src_ref=kacc.at[tx, 1 - c], dst_ref=cb.at[tx],
            send_sem=csend.at[tx], recv_sem=crecv.at[tx],
            device_id=(me, sib), device_id_type=MESH)

    def theirs(d, carry):
        tx = (x + d) % NX
        group(2, r2, tx, 1 - c)
        core_copy(tx).start()
        return carry

    def ours(d, carry):
        group(2, r2, (x + d) % NX, c)
        return carry

    lax.fori_loop(1, NX + 1, theirs, 0)
    lax.fori_loop(1, NX + 1, ours, 0)

    for dx in range(1, NX + 1):
        tx = (x + dx) % NX
        core_copy(tx).wait_recv()
        xs[tx] = kacc[tx, c] + cb[tx]
        if dx < NX:
            pltpu.make_async_remote_copy(
                src_ref=xs.at[tx], dst_ref=xb.at[x], send_sem=tsend.at[0], recv_sem=trecv.at[0],
                device_id=(me, tx * NC + c), device_id_type=MESH).start()

    wait_for(xb.at[pl.ds(0, NX - 1)], trecv.at[0])
    for dy in range(1, NY + 1):
        ty = (y + dy) % NY
        total = xs[x, :, ty]
        for dx in range(1, NX):
            total += xb[(x + dx) % NX, :, ty]
        ys[ty] = total
        if dy < NY:
            pltpu.make_async_remote_copy(
                src_ref=ys.at[ty], dst_ref=yb.at[y], send_sem=tsend.at[1], recv_sem=trecv.at[1],
                device_id=(ty * NZ + z, fk), device_id_type=MESH).start()

    wait_for(yb.at[pl.ds(0, NY - 1)], trecv.at[1])
    total = ys[y]
    for dy in range(1, NY):
        total += yb[(y + dy) % NY]
    vb[...] = total
    for m in range(NZ):
        zs[m] = vb[:, m, :]

    def z_send(d, carry):
        tz = (z + d) % NZ
        pltpu.make_async_remote_copy(
            src_ref=zs.at[tz], dst_ref=zb.at[z], send_sem=tsend.at[2], recv_sem=trecv.at[2],
            device_id=(y * NZ + tz, fk), device_id_type=MESH).start()
        return carry

    lax.fori_loop(1, NZ, z_send, 0)
    zb[z] = zs[z]
    wait_for(zb.at[pl.ds(0, NZ - 1)], trecv.at[2])
    result = jnp.sum(zb[...], axis=0) * factor
    out_ref[0:8, :] = result[:, :BS]
    out_ref[8:16, :] = result[:, BS:]

    for w, g, xsel in ((0, g0, x0), (1, g1, x1)):
        wait_for(g.at[pl.ds(0, NZ - 1)], gsend.at[3 * w])
        wait_for(g.at[pl.ds(0, (NY - 1) * NZ)], gsend.at[3 * w + 1])
        for _ in range(NX - 1):
            wait_for(xsel, gsend.at[3 * w + 2])
    for o, r_ref in ((0, r0), (1, r1), (2, r2)):
        wait_for(r_ref.at[pl.ds(0, NAUX_DEV - 1)], asend.at[o])
    for tx in range(NX):
        wait_for(cb.at[tx], csend.at[tx])
    wait_for(xb.at[pl.ds(0, NX - 1)], tsend.at[0])
    wait_for(yb.at[pl.ds(0, NY - 1)], tsend.at[1])
    wait_for(zb.at[pl.ds(0, NZ - 1)], tsend.at[2])


def per_device(three_index, col_blocks, pair_mask, occ_coef, occ_mask, kept):
    fock_count = lax.axis_size("fock")
    naux, rows, width = three_index.shape
    factor = float(naux * fock_count * occ_coef.shape[1]) ** (-0.5)
    bf, f32 = jnp.bfloat16, jnp.float32
    smem = pl.BlockSpec(memory_space=pltpu.SMEM)
    vmem = pl.BlockSpec(memory_space=pltpu.VMEM)
    dma = pltpu.SemaphoreType.DMA
    g = pltpu.VMEM((NAUX_DEV, 16, CHUNK), bf)
    xsel = pltpu.VMEM((SLOTS, 16, CHUNK), bf)
    wt = pltpu.VMEM((SLOTS, NX, 16, CHUNK), bf)
    send = pltpu.VMEM((NY, NZ, BS, CHUNK), bf)
    recv = pltpu.VMEM((NAUX_DEV, BS, CHUNK), bf)
    body = lambda *refs: kernel(factor, *refs)
    return pl.pallas_call(
        body,
        out_shape=jax.ShapeDtypeStruct((16, BS), f32),
        in_specs=[pl.BlockSpec(memory_space=pl.ANY), smem, smem, vmem, smem, smem],
        out_specs=vmem,
        scratch_shapes=[
            pltpu.VMEM((NY, NZ, rows, width), bf),
            pltpu.VMEM((CHUNKS, NX, 16, CHUNK), bf),
            g, g, xsel, xsel, wt, wt, wt, send, send, send, recv, recv, recv,
            pltpu.VMEM((NX, NC, 8, NY, 16, 2 * BS), f32),
            pltpu.VMEM((NX, 8, NY, 16, 2 * BS), f32),
            pltpu.VMEM((NX, 8, NY, 16, 2 * BS), f32),
            pltpu.VMEM((NX, 8, NY, 16, 2 * BS), f32),
            pltpu.VMEM((NY, 8, 16, 2 * BS), f32),
            pltpu.VMEM((NY, 8, 16, 2 * BS), f32),
            pltpu.VMEM((8, 16, 2 * BS), f32),
            pltpu.VMEM((NZ, 8, 2 * BS), f32),
            pltpu.VMEM((NZ, 8, 2 * BS), f32),
            dma, dma((7,)), dma((7,)), dma((3,)), dma((3,)), dma((4,)), dma((4,)), dma((3,)), dma((3,)),
        ],
        compiler_params=pltpu.CompilerParams(
            collective_id=0, has_side_effects=True, vmem_limit_bytes=40 * 2**20),
        cost_estimate=pl.CostEstimate(flops=2_400_000_000, bytes_accessed=8_000_000, transcendentals=0),
    )(three_index.reshape(NY, NZ, rows, width), col_blocks, pair_mask, occ_coef, occ_mask, kept)


def solution(mesh):
    in_specs = (P("fock", "aux", None), P(), P(), P("aux", None), P(), P())
    out_specs = P("fock", "aux")
    return jax.shard_map(
        per_device, mesh=mesh, in_specs=in_specs, out_specs=out_specs, check_vma=False
    )
```

```python
import jax
import jax.numpy as jnp
from jax import lax
from jax.experimental import pallas as pl
from jax.experimental.pallas import tpu as pltpu
from jax.sharding import PartitionSpec as P

MESH = pl.DeviceIdType.MESH
NY, NZ, NX, NC = 4, 16, 4, 2
NAUX_DEV = NY * NZ
BS = 64
SLOTS = 8
CHUNK = 128
CHUNKS = 3


def wait_for(ref, sem):
    pltpu.make_async_copy(ref, ref, sem).wait()


def kernel(factor, three_ref, colb_ref, pmask_ref, coef_ref, omask_ref, kept_ref, out_ref,
           tri, masked, g0, g1, ysel0, ysel1, yrec0, yrec1, x0, x1, w0, w1, w2, s0, s1, s2, r0, r1, r2,
           kacc, cb, xs, xb, ys, yb, early, kst, cb2, a1s, a1r, b1s, b1r, a2s, a2r, b2s, b2r, vb, zs, zb,
           tsem, gsend, grecv, asend, arecv, csend, crecv, c2send, c2recv, tsend, trecv):
    me = lax.axis_index("aux")
    fk = lax.axis_index("fock")
    y, z = me // NZ, me % NZ
    x, c = fk // NC, fk % NC
    sib = x * NC + (1 - c)

    load = pltpu.make_async_copy(three_ref, tri, tsem)
    load.start()

    bar = pltpu.get_barrier_semaphore()

    def greet(d, carry):
        pl.semaphore_signal(bar, inc=1, device_id=(y * NZ + (z + d) % NZ, fk), device_id_type=MESH)
        return carry

    lax.fori_loop(1, NZ, greet, 0)
    for dy in range(1, NY):
        pl.semaphore_signal(bar, inc=1, device_id=(((y + dy) % NY) * NZ + z, fk), device_id_type=MESH)
    for dx in range(1, NX):
        pl.semaphore_signal(bar, inc=1, device_id=(me, ((x + dx) % NX) * NC + c), device_id_type=MESH)
    pl.semaphore_signal(bar, inc=1, device_id=(me, sib), device_id_type=MESH)

    lane = lax.broadcasted_iota(jnp.int32, (BS, CHUNK), 1)
    for j in range(CHUNKS):
        m_lo = omask_ref[2 * j, me].astype(jnp.float32)
        m_hi = omask_ref[2 * j + 1, me].astype(jnp.float32)
        keep = jnp.where(lane < BS, m_lo, m_hi)
        part = coef_ref[:, j * CHUNK:(j + 1) * CHUNK].astype(jnp.float32) * keep
        masked[j] = part.astype(jnp.bfloat16).reshape(NX, 16, CHUNK)

    pl.semaphore_wait(bar, NZ - 1 + NY - 1 + NX - 1 + 1)

    def z_stage(w, g, chunk):
        def send(d, carry):
            tz = (z + d) % NZ
            pltpu.make_async_remote_copy(
                src_ref=masked.at[chunk, x], dst_ref=g.at[z],
                send_sem=gsend.at[3 * w], recv_sem=grecv.at[3 * w],
                device_id=(y * NZ + tz, fk), device_id_type=MESH).start()
            return carry
        lax.fori_loop(1, NZ, send, 0)
        g[z] = masked[chunk, x]

    def y_stage(w, g, ysel, yrec):
        wait_for(g.at[pl.ds(0, NZ - 1)], grecv.at[3 * w])
        for dy in range(1, NY + 1):
            ty = (y + dy) % NY
            for s in range(SLOTS):
                col = colb_ref[s, ty * NZ + z]
                here = jnp.where(col // NZ == y, pmask_ref[s, ty * NZ + z], 0).astype(jnp.float32)
                piece = (g[col % NZ].astype(jnp.float32) * here).astype(jnp.bfloat16)
                if dy < NY:
                    ysel[ty, s] = piece
                else:
                    yrec[y, s] = piece
            if dy < NY:
                pltpu.make_async_remote_copy(
                    src_ref=ysel.at[ty], dst_ref=yrec.at[y],
                    send_sem=gsend.at[3 * w + 1], recv_sem=grecv.at[3 * w + 1],
                    device_id=(ty * NZ + z, fk), device_id_type=MESH).start()

    def x_stage(w, yrec, xsel, wt):
        wait_for(yrec.at[pl.ds(0, NY - 1)], grecv.at[3 * w + 1])
        piece = yrec[0].astype(jnp.float32)
        for sy in range(1, NY):
            piece += yrec[sy].astype(jnp.float32)
        piece = piece.astype(jnp.bfloat16)
        xsel[...] = piece
        wt[:, x] = piece
        for dx in range(1, NX):
            tx = (x + dx) % NX
            pltpu.make_async_remote_copy(
                src_ref=xsel, dst_ref=wt.at[:, x],
                send_sem=gsend.at[3 * w + 2], recv_sem=grecv.at[3 * w + 2],
                device_id=(me, tx * NC + c), device_id_type=MESH).start()

    def x_wait(w, wt):
        wait_for(wt.at[:, pl.ds(0, NX - 1)], grecv.at[3 * w + 2])

    def chunk_out(o, wt, s_ref, r_ref):
        def product(tz):
            rows = tri[:, tz].reshape(NY * BS, SLOTS * BS)
            weights = wt[...].reshape(SLOTS * BS, CHUNK)
            half = jnp.dot(rows, weights, preferred_element_type=jnp.float32)
            s_ref[:, tz] = half.astype(jnp.bfloat16).reshape(NY, BS, CHUNK)

        def send(ty, tz):
            pltpu.make_async_remote_copy(
                src_ref=s_ref.at[ty, tz], dst_ref=r_ref.at[me],
                send_sem=asend.at[o], recv_sem=arecv.at[o],
                device_id=(ty * NZ + tz, fk), device_id_type=MESH).start()

        def step(q, carry):
            dz = ((q + 1) // 2) * (2 * (q % 2) - 1)
            tz = (z + dz + NZ) % NZ
            product(tz)
            for dy in range(NY):
                send((y + dy) % NY, tz)
            return carry

        lax.fori_loop(1, NZ, step, 0)
        product(z)
        for dy in range(1, NY):
            send((y + dy) % NY, z)
        r_ref[me] = s_ref[y, z]

    pair_lane = lax.broadcasted_iota(jnp.int32, (BS, 2 * BS), 1)

    def group(r_ref, tx, tc, store):
        base = (tx * NC + tc) * 16
        for j in range(8):
            lo, hi = base + j, base + 8 + j
            left = jnp.concatenate([r_ref[kept_ref[0, lo]], r_ref[kept_ref[0, hi]]], axis=0)
            right = jnp.concatenate([r_ref[kept_ref[1, lo]], r_ref[kept_ref[1, hi]]], axis=0)
            both = lax.dot_general(left, right, (((1,), (1,)), ((), ())), preferred_element_type=jnp.float32)
            store(j, jnp.where(pair_lane < BS, both[:BS], both[BS:]).reshape(NY, 16, 2 * BS))

    z_stage(0, g0, c)
    z_stage(1, g1, 2)
    y_stage(0, g0, ysel0, yrec0)
    y_stage(1, g1, ysel1, yrec1)
    x_stage(0, yrec0, x0, w0)
    load.wait()
    x_wait(0, w0)
    swap = pltpu.make_async_remote_copy(
        src_ref=w0, dst_ref=w1, send_sem=gsend.at[6], recv_sem=grecv.at[6],
        device_id=(me, sib), device_id_type=MESH)
    swap.start()
    chunk_out(0, w0, s0, r0)
    x_stage(1, yrec1, x1, w2)
    swap.wait()
    chunk_out(1, w1, s1, r1)
    x_wait(1, w2)
    chunk_out(2, w2, s2, r2)

    for o, r_ref in ((0, r0), (1, r1)):
        wait_for(r_ref.at[pl.ds(0, NAUX_DEV - 1)], arecv.at[o])

        def all_groups(t, carry):
            tx, tc = t // NC, t % NC

            def store(j, pick):
                if o == 0:
                    kacc[tx, tc, j] = pick
                else:
                    kacc[tx, tc, j] += pick

            group(r_ref, tx, tc, store)
            return carry

        lax.fori_loop(0, NX * NC, all_groups, 0)

    def core_copy(tx):
        return pltpu.make_async_remote_copy(
            src_ref=kacc.at[tx, 1 - c], dst_ref=cb.at[tx],
            send_sem=csend.at[tx], recv_sem=crecv.at[tx],
            device_id=(me, sib), device_id_type=MESH)

    for dx in range(1, NX + 1):
        core_copy((x + dx) % NX).start()
    for dx in range(1, NX + 1):
        tx = (x + dx) % NX
        core_copy(tx).wait_recv()
        xs[tx] = kacc[tx, c] + cb[tx]
        if dx < NX:
            pltpu.make_async_remote_copy(
                src_ref=xs.at[tx], dst_ref=xb.at[x], send_sem=tsend.at[0], recv_sem=trecv.at[0],
                device_id=(me, tx * NC + c), device_id_type=MESH).start()

    wait_for(xb.at[pl.ds(0, NX - 1)], trecv.at[0])
    for dy in range(1, NY + 1):
        ty = (y + dy) % NY
        total = xs[x, :, ty]
        for dx in range(1, NX):
            total += xb[(x + dx) % NX, :, ty]
        ys[ty] = total
        if dy < NY:
            pltpu.make_async_remote_copy(
                src_ref=ys.at[ty], dst_ref=yb.at[y], send_sem=tsend.at[1], recv_sem=trecv.at[1],
                device_id=(ty * NZ + z, fk), device_id_type=MESH).start()

    wait_for(yb.at[pl.ds(0, NY - 1)], trecv.at[1])
    total = ys[y]
    for dy in range(1, NY):
        total += yb[(y + dy) % NY]
    early[...] = total
    for tx in range(NX):
        wait_for(cb.at[tx], csend.at[tx])

    wait_for(r2.at[pl.ds(0, NAUX_DEV - 1)], arecv.at[2])

    def core_copy2(tx):
        return pltpu.make_async_remote_copy(
            src_ref=kst.at[tx], dst_ref=cb2.at[tx],
            send_sem=c2send.at[tx], recv_sem=c2recv.at[tx],
            device_id=(me, sib), device_id_type=MESH)

    def theirs(d, carry):
        tx = (x + d) % NX

        def store(j, pick):
            kst[tx, j] = pick.astype(jnp.bfloat16)

        group(r2, tx, 1 - c, store)
        core_copy2(tx).start()
        return carry

    lax.fori_loop(1, NX + 1, theirs, 0)

    def ours(tx):
        def store(j, pick):
            kacc[tx, c, j] = pick

        group(r2, tx, c, store)
        core_copy2(tx).wait_recv()
        for half in range(2):
            pick = kacc[tx, c, half * 4:half * 4 + 4] + cb2[tx, half * 4:half * 4 + 4].astype(jnp.float32)
            pick = pick.astype(jnp.bfloat16)
            if half == 0:
                a1s[tx] = pick
            else:
                for ty in range(NY):
                    b1s[ty, tx] = pick[:, ty]

    def send_y(tx):
        for dy in range(1, NY):
            ty = (y + dy) % NY
            pltpu.make_async_remote_copy(
                src_ref=b1s.at[ty, tx], dst_ref=b1r.at[y, tx], send_sem=tsend.at[3], recv_sem=trecv.at[3],
                device_id=(ty * NZ + z, fk), device_id_type=MESH).start()

    def ours_step(d, carry):
        tx = (x + d) % NX
        ours(tx)
        pltpu.make_async_remote_copy(
            src_ref=a1s.at[tx], dst_ref=a1r.at[x], send_sem=tsend.at[2], recv_sem=trecv.at[2],
            device_id=(me, tx * NC + c), device_id_type=MESH).start()
        send_y(tx)
        return carry

    lax.fori_loop(1, NX, ours_step, 0)
    ours(x)
    send_y(x)

    wait_for(a1r.at[pl.ds(0, NX - 1)], trecv.at[2])
    for dy in range(1, NY + 1):
        ty = (y + dy) % NY
        total = a1s[x, :, ty].astype(jnp.float32)
        for dx in range(1, NX):
            total += a1r[(x + dx) % NX, :, ty].astype(jnp.float32)
        if dy < NY:
            a2s[ty] = total.astype(jnp.bfloat16)
            pltpu.make_async_remote_copy(
                src_ref=a2s.at[ty], dst_ref=a2r.at[y], send_sem=tsend.at[4], recv_sem=trecv.at[4],
                device_id=(ty * NZ + z, fk), device_id_type=MESH).start()
        else:
            vb[0:4] = total + early[0:4]

    wait_for(b1r.at[pl.ds(0, NY - 1)], trecv.at[3])
    for dx in range(1, NX + 1):
        tx = (x + dx) % NX
        total = b1s[y, tx].astype(jnp.float32)
        for dy in range(1, NY):
            total += b1r[(y + dy) % NY, tx].astype(jnp.float32)
        if dx < NX:
            b2s[tx] = total.astype(jnp.bfloat16)
            pltpu.make_async_remote_copy(
                src_ref=b2s.at[tx], dst_ref=b2r.at[x], send_sem=tsend.at[5], recv_sem=trecv.at[5],
                device_id=(me, tx * NC + c), device_id_type=MESH).start()
        else:
            vb[4:8] = total + early[4:8]

    wait_for(a2r.at[pl.ds(0, NY - 1)], trecv.at[4])
    total = vb[0:4]
    for dy in range(1, NY):
        total += a2r[(y + dy) % NY].astype(jnp.float32)
    vb[0:4] = total
    wait_for(b2r.at[pl.ds(0, NX - 1)], trecv.at[5])
    total = vb[4:8]
    for dx in range(1, NX):
        total += b2r[(x + dx) % NX].astype(jnp.float32)
    vb[4:8] = total
    for m in range(NZ):
        zs[m] = vb[:, m, :]

    def z_send(d, carry):
        tz = (z + d) % NZ
        pltpu.make_async_remote_copy(
            src_ref=zs.at[tz], dst_ref=zb.at[z], send_sem=tsend.at[6], recv_sem=trecv.at[6],
            device_id=(y * NZ + tz, fk), device_id_type=MESH).start()
        return carry

    lax.fori_loop(1, NZ, z_send, 0)
    zb[z] = zs[z]
    wait_for(zb.at[pl.ds(0, NZ - 1)], trecv.at[6])
    result = jnp.sum(zb[...], axis=0) * factor
    out_ref[0:8, :] = result[:, :BS]
    out_ref[8:16, :] = result[:, BS:]

    for w, g, yrec, xsel in ((0, g0, yrec0, x0), (1, g1, yrec1, x1)):
        wait_for(g.at[pl.ds(0, NZ - 1)], gsend.at[3 * w])
        wait_for(yrec.at[pl.ds(0, NY - 1)], gsend.at[3 * w + 1])
        for _ in range(NX - 1):
            wait_for(xsel, gsend.at[3 * w + 2])
    for o, r_ref in ((0, r0), (1, r1), (2, r2)):
        wait_for(r_ref.at[pl.ds(0, NAUX_DEV - 1)], asend.at[o])
    for tx in range(NX):
        wait_for(cb2.at[tx], c2send.at[tx])
    wait_for(xb.at[pl.ds(0, NX - 1)], tsend.at[0])
    wait_for(yb.at[pl.ds(0, NY - 1)], tsend.at[1])
    wait_for(a1r.at[pl.ds(0, NX - 1)], tsend.at[2])
    wait_for(b1r.at[pl.ds(0, NY - 1)], tsend.at[3])
    wait_for(a2r.at[pl.ds(0, NY - 1)], tsend.at[4])
    wait_for(b2r.at[pl.ds(0, NX - 1)], tsend.at[5])
    wait_for(zb.at[pl.ds(0, NZ - 1)], tsend.at[6])


def per_device(three_index, col_blocks, pair_mask, occ_coef, occ_mask, kept):
    fock_count = lax.axis_size("fock")
    naux, rows, width = three_index.shape
    factor = float(naux * fock_count * occ_coef.shape[1]) ** (-0.5)
    bf, f32 = jnp.bfloat16, jnp.float32
    smem = pl.BlockSpec(memory_space=pltpu.SMEM)
    vmem = pl.BlockSpec(memory_space=pltpu.VMEM)
    dma = pltpu.SemaphoreType.DMA
    g = pltpu.VMEM((NZ, 16, CHUNK), bf)
    ysel = pltpu.VMEM((NY, SLOTS, 16, CHUNK), bf)
    xsel = pltpu.VMEM((SLOTS, 16, CHUNK), bf)
    wt = pltpu.VMEM((SLOTS, NX, 16, CHUNK), bf)
    send = pltpu.VMEM((NY, NZ, BS, CHUNK), bf)
    recv = pltpu.VMEM((NAUX_DEV, BS, CHUNK), bf)
    first = pltpu.VMEM((4, 4, 4, 16, 2 * BS), bf)
    second = pltpu.VMEM((4, 4, 16, 2 * BS), bf)
    body = lambda *refs: kernel(factor, *refs)
    return pl.pallas_call(
        body,
        out_shape=jax.ShapeDtypeStruct((16, BS), f32),
        in_specs=[pl.BlockSpec(memory_space=pl.ANY), smem, smem, vmem, smem, smem],
        out_specs=vmem,
        scratch_shapes=[
            pltpu.VMEM((NY, NZ, rows, width), bf),
            pltpu.VMEM((CHUNKS, NX, 16, CHUNK), bf),
            g, g, ysel, ysel, ysel, ysel, xsel, xsel, wt, wt, wt, send, send, send, recv, recv, recv,
            pltpu.VMEM((NX, NC, 8, NY, 16, 2 * BS), f32),
            pltpu.VMEM((NX, 8, NY, 16, 2 * BS), f32),
            pltpu.VMEM((NX, 8, NY, 16, 2 * BS), f32),
            pltpu.VMEM((NX, 8, NY, 16, 2 * BS), f32),
            pltpu.VMEM((NY, 8, 16, 2 * BS), f32),
            pltpu.VMEM((NY, 8, 16, 2 * BS), f32),
            pltpu.VMEM((8, 16, 2 * BS), f32),
            pltpu.VMEM((NX, 8, NY, 16, 2 * BS), bf),
            pltpu.VMEM((NX, 8, NY, 16, 2 * BS), bf),
            first, first, first, first, second, second, second, second,
            pltpu.VMEM((8, 16, 2 * BS), f32),
            pltpu.VMEM((NZ, 8, 2 * BS), f32),
            pltpu.VMEM((NZ, 8, 2 * BS), f32),
            dma, dma((7,)), dma((7,)), dma((3,)), dma((3,)), dma((4,)), dma((4,)), dma((4,)), dma((4,)),
            dma((7,)), dma((7,)),
        ],
        compiler_params=pltpu.CompilerParams(
            collective_id=0, has_side_effects=True, vmem_limit_bytes=62 * 2**20),
        cost_estimate=pl.CostEstimate(flops=2_400_000_000, bytes_accessed=8_000_000, transcendentals=0),
    )(three_index.reshape(NY, NZ, rows, width), col_blocks.T, pair_mask.T, occ_coef, occ_mask.T, kept.T)


def solution(mesh):
    in_specs = (P("fock", "aux", None), P(), P(), P("aux", None), P(), P())
    out_specs = P("fock", "aux")
    return jax.shard_map(
        per_device, mesh=mesh, in_specs=in_specs, out_specs=out_specs, check_vma=False
    )
```

```python
import jax
import jax.numpy as jnp
from jax import lax
from jax.experimental import pallas as pl
from jax.experimental.pallas import tpu as pltpu
from jax.sharding import PartitionSpec as P

MESH = pl.DeviceIdType.MESH
NY, NZ, NX, NC = 4, 16, 4, 2
NAUX_DEV = NY * NZ
BS = 64
SLOTS = 8
CHUNK = 128
CHUNKS = 3


def wait_for(ref, sem):
    pltpu.make_async_copy(ref, ref, sem).wait()


def kernel(factor, three_ref, colb_hbm, pmask_hbm, coef_hbm, omask_hbm, kept_hbm, out_ref,
           colb_ref, pmask_ref, coef_ref, omask_ref, kept_ref, isem, tri, masked, g0, g1, ysel0, ysel1, yrec0, yrec1, x0, x1, w0, w1, w2, w3, s0, s1, s2, r0, r1, r2,
           kacc, cb, xs, xb, ys, yb, early, kst, cb2, a1s, a1r, b1s, b1r, a2s, a2r, b2s, b2r, vb, zs, zb,
           tsem, gsend, grecv, asend, arecv, csend, crecv, c2send, c2recv, tsend, trecv):
    me = lax.axis_index("aux")
    fk = lax.axis_index("fock")
    y, z = me // NZ, me % NZ
    x, c = fk // NC, fk % NC
    sib = x * NC + (1 - c)

    def away(q):
        return (z + ((q + 1) // 2) * (2 * (q % 2) - 1) + NZ) % NZ

    def far_first(q):
        return away(NZ - q)

    loads = [
        pltpu.make_async_copy(src, dst, isem.at[k])
        for k, (src, dst) in enumerate((
            (omask_hbm, omask_ref), (coef_hbm, coef_ref), (colb_hbm, colb_ref),
            (pmask_hbm, pmask_ref), (kept_hbm, kept_ref)))
    ]
    for copy in loads:
        copy.start()

    bar = pltpu.get_barrier_semaphore()

    def greet(d, carry):
        pl.semaphore_signal(bar, inc=1, device_id=(y * NZ + far_first(d), fk), device_id_type=MESH)
        return carry

    lax.fori_loop(1, NZ, greet, 0)
    for dy in range(1, NY):
        pl.semaphore_signal(bar, inc=1, device_id=(((y + dy) % NY) * NZ + z, fk), device_id_type=MESH)
    for dx in range(1, NX):
        pl.semaphore_signal(bar, inc=1, device_id=(me, ((x + dx) % NX) * NC + c), device_id_type=MESH)
    pl.semaphore_signal(bar, inc=1, device_id=(me, sib), device_id_type=MESH)

    load = pltpu.make_async_copy(three_ref, tri, tsem)
    load.start()
    for copy in loads:
        copy.wait()

    lane = lax.broadcasted_iota(jnp.int32, (BS, CHUNK), 1)
    for j in range(CHUNKS):
        m_lo = omask_ref[2 * j, me].astype(jnp.float32)
        m_hi = omask_ref[2 * j + 1, me].astype(jnp.float32)
        keep = jnp.where(lane < BS, m_lo, m_hi)
        part = coef_ref[:, j * CHUNK:(j + 1) * CHUNK].astype(jnp.float32) * keep
        masked[j] = part.astype(jnp.bfloat16).reshape(NX, 16, CHUNK)

    pl.semaphore_wait(bar, NZ - 1 + NY - 1 + NX - 1 + 1)

    def z_send_coef(w, g, chunk, slot):
        def send(d, carry):
            tz = far_first(d)
            pltpu.make_async_remote_copy(
                src_ref=masked.at[chunk, x], dst_ref=g.at[slot],
                send_sem=gsend.at[3 * w], recv_sem=grecv.at[3 * w],
                device_id=(y * NZ + tz, fk), device_id_type=MESH).start()
            return carry
        lax.fori_loop(1, NZ, send, 0)
        g[slot] = masked[chunk, x]

    def y_stage(w, g, ysel, yrec):
        for dy in (2, 1, 3, NY):
            ty = (y + dy) % NY
            for s in range(SLOTS):
                col = colb_ref[s, ty * NZ + z]
                flag = pmask_ref[s, ty * NZ + z]
                if w == 1:
                    flag = jnp.where(col % 2 == c, flag, 0)
                here = jnp.where(col // NZ == y, flag, 0).astype(jnp.float32).astype(jnp.bfloat16)
                piece = g[col % NZ // (1 + w)] * here
                if dy < NY:
                    ysel[ty, s] = piece
                else:
                    yrec[y, s] = piece
            if dy < NY:
                pltpu.make_async_remote_copy(
                    src_ref=ysel.at[ty], dst_ref=yrec.at[y],
                    send_sem=gsend.at[3 * w + 1], recv_sem=grecv.at[3 * w + 1],
                    device_id=(ty * NZ + z, fk), device_id_type=MESH).start()

    def x_stage(w, yrec, xsel, wt):
        wait_for(yrec.at[pl.ds(0, NY - 1)], grecv.at[3 * w + 1])
        piece = yrec[0].astype(jnp.float32)
        for sy in range(1, NY):
            piece += yrec[sy].astype(jnp.float32)
        piece = piece.astype(jnp.bfloat16)
        xsel[...] = piece
        wt[:, x] = piece
        for dx in (2, 1, 3):
            tx = (x + dx) % NX
            pltpu.make_async_remote_copy(
                src_ref=xsel, dst_ref=wt.at[:, x],
                send_sem=gsend.at[3 * w + 2], recv_sem=grecv.at[3 * w + 2],
                device_id=(me, tx * NC + c), device_id_type=MESH).start()

    def x_wait(w, wt):
        wait_for(wt.at[:, pl.ds(0, NX - 1)], grecv.at[3 * w + 2])

    def chunk_out(o, wt, s_ref, r_ref):
        def product(tz):
            rows = tri[:, tz].reshape(NY * BS, SLOTS * BS)
            weights = wt[...].reshape(SLOTS * BS, CHUNK)
            half = jnp.dot(rows, weights, preferred_element_type=jnp.float32)
            s_ref[:, tz] = half.astype(jnp.bfloat16).reshape(NY, BS, CHUNK)

        def send(ty, tz):
            pltpu.make_async_remote_copy(
                src_ref=s_ref.at[ty, tz], dst_ref=r_ref.at[me],
                send_sem=asend.at[o], recv_sem=arecv.at[o],
                device_id=(ty * NZ + tz, fk), device_id_type=MESH).start()

        def step(q, carry):
            tz = far_first(q) if o == 2 else away(q)
            product(tz)
            for dy in range(NY):
                send((y + dy) % NY, tz)
            return carry

        lax.fori_loop(1, NZ, step, 0)
        product(z)
        for dy in range(1, NY):
            send((y + dy) % NY, z)
        r_ref[me] = s_ref[y, z]

    pair_lane = lax.broadcasted_iota(jnp.int32, (BS, 2 * BS), 1)

    def group(r_ref, tx, tc, store):
        base = (tx * NC + tc) * 16
        for j in range(8):
            lo, hi = base + j, base + 8 + j
            left = jnp.concatenate([r_ref[kept_ref[0, lo]], r_ref[kept_ref[0, hi]]], axis=0)
            right = jnp.concatenate([r_ref[kept_ref[1, lo]], r_ref[kept_ref[1, hi]]], axis=0)
            both = lax.dot_general(left, right, (((1,), (1,)), ((), ())), preferred_element_type=jnp.float32)
            store(j, jnp.where(pair_lane < BS, both[:BS], both[BS:]).reshape(NY, 16, 2 * BS))

    mine = z % 2 == c
    z_send_coef(0, g0, c, z)

    @pl.when(mine)
    def _():
        z_send_coef(1, g1, 2, z // 2)

    wait_for(g0.at[pl.ds(0, NZ - 1)], grecv.at[0])
    y_stage(0, g0, ysel0, yrec0)
    x_stage(0, yrec0, x0, w0)

    @pl.when(mine)
    def _():
        wait_for(g1.at[pl.ds(0, NZ // 2 - 1)], grecv.at[3])

    @pl.when(jnp.logical_not(mine))
    def _():
        wait_for(g1, grecv.at[3])

    y_stage(1, g1, ysel1, yrec1)
    load.wait()
    x_wait(0, w0)
    swap = pltpu.make_async_remote_copy(
        src_ref=w0, dst_ref=w1, send_sem=gsend.at[6], recv_sem=grecv.at[6],
        device_id=(me, sib), device_id_type=MESH)
    swap.start()
    chunk_out(0, w0, s0, r0)
    x_stage(1, yrec1, x1, w2)
    swap.wait()
    chunk_out(1, w1, s1, r1)
    x_wait(1, w2)
    merge = pltpu.make_async_remote_copy(
        src_ref=w2, dst_ref=w3, send_sem=gsend.at[7], recv_sem=grecv.at[7],
        device_id=(me, sib), device_id_type=MESH)
    merge.start()
    merge.wait()
    w2[...] = (w2[...].astype(jnp.float32) + w3[...].astype(jnp.float32)).astype(jnp.bfloat16)
    chunk_out(2, w2, s2, r2)

    for o, r_ref in ((0, r0), (1, r1)):
        wait_for(r_ref.at[pl.ds(0, NAUX_DEV - 1)], arecv.at[o])

        def all_groups(t, carry):
            tx, tc = t // NC, t % NC

            def store(j, pick):
                if o == 0:
                    kacc[tx, tc, j] = pick
                else:
                    kacc[tx, tc, j] += pick

            group(r_ref, tx, tc, store)
            return carry

        lax.fori_loop(0, NX * NC, all_groups, 0)

    def core_copy(tx):
        return pltpu.make_async_remote_copy(
            src_ref=kacc.at[tx, 1 - c], dst_ref=cb.at[tx],
            send_sem=csend.at[tx], recv_sem=crecv.at[tx],
            device_id=(me, sib), device_id_type=MESH)

    for dx in range(1, NX + 1):
        core_copy((x + dx) % NX).start()
    for dx in range(1, NX + 1):
        tx = (x + dx) % NX
        core_copy(tx).wait_recv()
        xs[tx] = kacc[tx, c] + cb[tx]
        if dx < NX:
            pltpu.make_async_remote_copy(
                src_ref=xs.at[tx], dst_ref=xb.at[x], send_sem=tsend.at[0], recv_sem=trecv.at[0],
                device_id=(me, tx * NC + c), device_id_type=MESH).start()

    wait_for(xb.at[pl.ds(0, NX - 1)], trecv.at[0])
    for dy in range(1, NY + 1):
        ty = (y + dy) % NY
        total = xs[x, :, ty]
        for dx in range(1, NX):
            total += xb[(x + dx) % NX, :, ty]
        ys[ty] = total
        if dy < NY:
            pltpu.make_async_remote_copy(
                src_ref=ys.at[ty], dst_ref=yb.at[y], send_sem=tsend.at[1], recv_sem=trecv.at[1],
                device_id=(ty * NZ + z, fk), device_id_type=MESH).start()

    wait_for(yb.at[pl.ds(0, NY - 1)], trecv.at[1])
    total = ys[y]
    for dy in range(1, NY):
        total += yb[(y + dy) % NY]
    early[...] = total
    for tx in range(NX):
        wait_for(cb.at[tx], csend.at[tx])

    wait_for(r2.at[pl.ds(0, NAUX_DEV - 1)], arecv.at[2])

    def core_copy2(tx):
        return pltpu.make_async_remote_copy(
            src_ref=kst.at[tx], dst_ref=cb2.at[tx],
            send_sem=c2send.at[tx], recv_sem=c2recv.at[tx],
            device_id=(me, sib), device_id_type=MESH)

    def theirs(tx):
        def store(j, pick):
            kst[tx, j] = pick.astype(jnp.bfloat16)

        group(r2, tx, 1 - c, store)
        core_copy2(tx).start()

    def ours(tx):
        def store(j, pick):
            kacc[tx, c, j] = pick

        group(r2, tx, c, store)
        core_copy2(tx).wait_recv()
        for half in range(2):
            pick = kacc[tx, c, half * 4:half * 4 + 4] + cb2[tx, half * 4:half * 4 + 4].astype(jnp.float32)
            pick = pick.astype(jnp.bfloat16)
            if half == 0:
                a1s[tx] = pick
            else:
                for ty in range(NY):
                    b1s[ty, tx] = pick[:, ty]

    def send_y(tx):
        for dy in (2, 1, 3):
            ty = (y + dy) % NY
            pltpu.make_async_remote_copy(
                src_ref=b1s.at[ty, tx], dst_ref=b1r.at[y, tx], send_sem=tsend.at[3], recv_sem=trecv.at[3],
                device_id=(ty * NZ + z, fk), device_id_type=MESH).start()

    def both_step(d, carry):
        theirs((x + NX - 1 - d) % NX)
        tx = (x + NX - d) % NX
        ours(tx)
        pltpu.make_async_remote_copy(
            src_ref=a1s.at[tx], dst_ref=a1r.at[x], send_sem=tsend.at[2], recv_sem=trecv.at[2],
            device_id=(me, tx * NC + c), device_id_type=MESH).start()
        send_y(tx)
        return carry

    theirs((x + NX - 1) % NX)
    lax.fori_loop(1, NX, both_step, 0)
    ours(x)
    send_y(x)

    wait_for(a1r.at[pl.ds(0, NX - 1)], trecv.at[2])
    for dy in (2, 1, 3, NY):
        ty = (y + dy) % NY
        total = a1s[x, :, ty].astype(jnp.float32)
        for dx in range(1, NX):
            total += a1r[(x + dx) % NX, :, ty].astype(jnp.float32)
        if dy < NY:
            a2s[ty] = total.astype(jnp.bfloat16)
            pltpu.make_async_remote_copy(
                src_ref=a2s.at[ty], dst_ref=a2r.at[y], send_sem=tsend.at[4], recv_sem=trecv.at[4],
                device_id=(ty * NZ + z, fk), device_id_type=MESH).start()
        else:
            vb[0:4] = total + early[0:4]

    wait_for(b1r.at[pl.ds(0, NY - 1)], trecv.at[3])
    for dx in (2, 1, 3, NX):
        tx = (x + dx) % NX
        total = b1s[y, tx].astype(jnp.float32)
        for dy in range(1, NY):
            total += b1r[(y + dy) % NY, tx].astype(jnp.float32)
        if dx < NX:
            b2s[tx] = total.astype(jnp.bfloat16)
            pltpu.make_async_remote_copy(
                src_ref=b2s.at[tx], dst_ref=b2r.at[x], send_sem=tsend.at[5], recv_sem=trecv.at[5],
                device_id=(me, tx * NC + c), device_id_type=MESH).start()
        else:
            vb[4:8] = total + early[4:8]

    wait_for(a2r.at[pl.ds(0, NY - 1)], trecv.at[4])
    total = vb[0:4]
    for dy in range(1, NY):
        total += a2r[(y + dy) % NY].astype(jnp.float32)
    vb[0:4] = total
    wait_for(b2r.at[pl.ds(0, NX - 1)], trecv.at[5])
    total = vb[4:8]
    for dx in range(1, NX):
        total += b2r[(x + dx) % NX].astype(jnp.float32)
    vb[4:8] = total
    for m in range(NZ):
        zs[m] = vb[:, m, :]

    def z_send(d, carry):
        tz = far_first(d)
        pltpu.make_async_remote_copy(
            src_ref=zs.at[tz], dst_ref=zb.at[z], send_sem=tsend.at[6], recv_sem=trecv.at[6],
            device_id=(y * NZ + tz, fk), device_id_type=MESH).start()
        return carry

    lax.fori_loop(1, NZ, z_send, 0)
    zb[z] = zs[z]
    wait_for(zb.at[pl.ds(0, NZ - 1)], trecv.at[6])
    result = jnp.sum(zb[...], axis=0) * factor
    out_ref[0:8, :] = result[:, :BS]
    out_ref[8:16, :] = result[:, BS:]

    wait_for(g0.at[pl.ds(0, NZ - 1)], gsend.at[0])

    @pl.when(mine)
    def _():
        for rows in (NZ // 2, NZ // 2 - 1):
            wait_for(g1.at[pl.ds(0, rows)], gsend.at[3])

    for w, yrec, xsel in ((0, yrec0, x0), (1, yrec1, x1)):
        wait_for(yrec.at[pl.ds(0, NY - 1)], gsend.at[3 * w + 1])
        for _ in range(NX - 1):
            wait_for(xsel, gsend.at[3 * w + 2])
    for o, r_ref in ((0, r0), (1, r1), (2, r2)):
        wait_for(r_ref.at[pl.ds(0, NAUX_DEV - 1)], asend.at[o])
    for tx in range(NX):
        wait_for(cb2.at[tx], c2send.at[tx])
    wait_for(xb.at[pl.ds(0, NX - 1)], tsend.at[0])
    wait_for(yb.at[pl.ds(0, NY - 1)], tsend.at[1])
    wait_for(a1r.at[pl.ds(0, NX - 1)], tsend.at[2])
    wait_for(b1r.at[pl.ds(0, NY - 1)], tsend.at[3])
    wait_for(a2r.at[pl.ds(0, NY - 1)], tsend.at[4])
    wait_for(b2r.at[pl.ds(0, NX - 1)], tsend.at[5])
    wait_for(zb.at[pl.ds(0, NZ - 1)], tsend.at[6])


def per_device(three_index, col_blocks, pair_mask, occ_coef, occ_mask, kept):
    fock_count = lax.axis_size("fock")
    naux, rows, width = three_index.shape
    factor = float(naux * fock_count * occ_coef.shape[1]) ** (-0.5)
    bf, f32 = jnp.bfloat16, jnp.float32
    vmem = pl.BlockSpec(memory_space=pltpu.VMEM)
    dma = pltpu.SemaphoreType.DMA
    g = pltpu.VMEM((NZ, 16, CHUNK), bf)
    ysel = pltpu.VMEM((NY, SLOTS, 16, CHUNK), bf)
    xsel = pltpu.VMEM((SLOTS, 16, CHUNK), bf)
    wt = pltpu.VMEM((SLOTS, NX, 16, CHUNK), bf)
    send = pltpu.VMEM((NY, NZ, BS, CHUNK), bf)
    recv = pltpu.VMEM((NAUX_DEV, BS, CHUNK), bf)
    first = pltpu.VMEM((4, 4, 4, 16, 2 * BS), bf)
    second = pltpu.VMEM((4, 4, 16, 2 * BS), bf)
    body = lambda *refs: kernel(factor, *refs)
    return pl.pallas_call(
        body,
        out_shape=jax.ShapeDtypeStruct((16, BS), f32),
        in_specs=[pl.BlockSpec(memory_space=pl.ANY)] * 6,
        out_specs=vmem,
        scratch_shapes=[
            pltpu.SMEM((SLOTS, NAUX_DEV), jnp.int32),
            pltpu.SMEM((SLOTS, NAUX_DEV), jnp.int32),
            pltpu.VMEM(occ_coef.shape, bf),
            pltpu.SMEM((2 * CHUNKS, NAUX_DEV), jnp.int32),
            pltpu.SMEM((2, kept.shape[0]), jnp.int32),
            dma((5,)),
            pltpu.VMEM((NY, NZ, rows, width), bf),
            pltpu.VMEM((CHUNKS, NX, 16, CHUNK), bf),
            g, pltpu.VMEM((NZ // 2, 16, CHUNK), bf), ysel, ysel, ysel, ysel, xsel, xsel, wt, wt, wt, wt, send, send, send, recv, recv, recv,
            pltpu.VMEM((NX, NC, 8, NY, 16, 2 * BS), f32),
            pltpu.VMEM((NX, 8, NY, 16, 2 * BS), f32),
            pltpu.VMEM((NX, 8, NY, 16, 2 * BS), f32),
            pltpu.VMEM((NX, 8, NY, 16, 2 * BS), f32),
            pltpu.VMEM((NY, 8, 16, 2 * BS), f32),
            pltpu.VMEM((NY, 8, 16, 2 * BS), f32),
            pltpu.VMEM((8, 16, 2 * BS), f32),
            pltpu.VMEM((NX, 8, NY, 16, 2 * BS), bf),
            pltpu.VMEM((NX, 8, NY, 16, 2 * BS), bf),
            first, first, first, first, second, second, second, second,
            pltpu.VMEM((8, 16, 2 * BS), f32),
            pltpu.VMEM((NZ, 8, 2 * BS), f32),
            pltpu.VMEM((NZ, 8, 2 * BS), f32),
            dma, dma((8,)), dma((8,)), dma((3,)), dma((3,)), dma((4,)), dma((4,)), dma((4,)), dma((4,)),
            dma((7,)), dma((7,)),
        ],
        compiler_params=pltpu.CompilerParams(
            collective_id=0, has_side_effects=True, vmem_limit_bytes=62 * 2**20),
        cost_estimate=pl.CostEstimate(flops=2_400_000_000, bytes_accessed=8_000_000, transcendentals=0),
    )(three_index.reshape(NY, NZ, rows, width), col_blocks.T, pair_mask.T, occ_coef, occ_mask.T, kept.T)


def solution(mesh):
    in_specs = (P("fock", "aux", None), P(), P(), P("aux", None), P(), P())
    out_specs = P("fock", "aux")
    return jax.shard_map(
        per_device, mesh=mesh, in_specs=in_specs, out_specs=out_specs, check_vma=False
    )
```

```python
import jax
import jax.numpy as jnp
from jax import lax
from jax.experimental import pallas as pl
from jax.experimental.pallas import tpu as pltpu
from jax.sharding import PartitionSpec as P

MESH = pl.DeviceIdType.MESH
NY, NZ, NX, NC = 4, 16, 4, 2
NAUX_DEV = NY * NZ
BS = 64
SLOTS = 8
CHUNK = 128
CHUNKS = 3


def wait_for(ref, sem):
    pltpu.make_async_copy(ref, ref, sem).wait()


def kernel(three_ref, colb_hbm, pmask_hbm, coef_hbm, omask_hbm, kept_hbm, out_ref,
           colb_ref, pmask_ref, coef_ref, omask_ref, kept_ref, isem, tri, masked, g0, g1, ysel0, ysel1, yrec0, yrec1, x0, x1, w0, w1, w2, w3, s0, s1, s2, r0, r1, r2,
           kacc, cb, xs, xb, ys, yb, early, kst, cb2, a1s, a1r, b1s, b1r, a2s, a2r, b2s, b2r, vb, zs, zb,
           tsem, gsend, grecv, asend, arecv, csend, crecv, c2send, c2recv, tsend, trecv):
    me = lax.axis_index("aux")
    fk = lax.axis_index("fock")
    y, z = me // NZ, me % NZ
    x, c = fk // NC, fk % NC
    sib = x * NC + (1 - c)

    def away(q):
        return (z + ((q + 1) // 2) * (2 * (q % 2) - 1) + NZ) % NZ

    def far_first(q):
        return away(NZ - q)

    loads = [
        pltpu.make_async_copy(src, dst, isem.at[k])
        for k, (src, dst) in enumerate((
            (omask_hbm, omask_ref), (coef_hbm, coef_ref), (colb_hbm, colb_ref),
            (pmask_hbm, pmask_ref), (kept_hbm, kept_ref)))
    ]
    for copy in loads:
        copy.start()

    bar = pltpu.get_barrier_semaphore()

    def greet(d, carry):
        pl.semaphore_signal(bar, inc=1, device_id=(y * NZ + far_first(d), fk), device_id_type=MESH)
        return carry

    lax.fori_loop(1, NZ, greet, 0)
    for dy in range(1, NY):
        pl.semaphore_signal(bar, inc=1, device_id=(((y + dy) % NY) * NZ + z, fk), device_id_type=MESH)
    for dx in range(1, NX):
        pl.semaphore_signal(bar, inc=1, device_id=(me, ((x + dx) % NX) * NC + c), device_id_type=MESH)
    pl.semaphore_signal(bar, inc=1, device_id=(me, sib), device_id_type=MESH)

    load = pltpu.make_async_copy(three_ref, tri, tsem)
    load.start()
    for copy in loads:
        copy.wait()

    lane = lax.broadcasted_iota(jnp.int32, (BS, CHUNK), 1)
    for j in range(CHUNKS):
        m_lo = omask_ref[2 * j, me].astype(jnp.float32)
        m_hi = omask_ref[2 * j + 1, me].astype(jnp.float32)
        keep = jnp.where(lane < BS, m_lo, m_hi)
        part = coef_ref[:, j * CHUNK:(j + 1) * CHUNK].astype(jnp.float32) * keep
        masked[j] = part.astype(jnp.bfloat16).reshape(NX, 16, CHUNK)

    pl.semaphore_wait(bar, NZ - 1 + NY - 1 + NX - 1 + 1)

    def z_send_coef(w, g, chunk, slot):
        def send(d, carry):
            tz = far_first(d)
            pltpu.make_async_remote_copy(
                src_ref=masked.at[chunk, x], dst_ref=g.at[slot],
                send_sem=gsend.at[3 * w], recv_sem=grecv.at[3 * w],
                device_id=(y * NZ + tz, fk), device_id_type=MESH).start()
            return carry
        lax.fori_loop(1, NZ, send, 0)
        g[slot] = masked[chunk, x]

    def y_stage(w, g, ysel, yrec):
        for dy in (2, 1, 3, NY):
            ty = (y + dy) % NY
            for s in range(SLOTS):
                col = colb_ref[s, ty * NZ + z]
                flag = pmask_ref[s, ty * NZ + z]
                if w == 1:
                    flag = jnp.where(col % 2 == c, flag, 0)
                here = jnp.where(col // NZ == y, flag, 0).astype(jnp.float32).astype(jnp.bfloat16)
                piece = g[col % NZ // (1 + w)] * here
                if dy < NY:
                    ysel[ty, s] = piece
                else:
                    yrec[y, s] = piece
            if dy < NY:
                pltpu.make_async_remote_copy(
                    src_ref=ysel.at[ty], dst_ref=yrec.at[y],
                    send_sem=gsend.at[3 * w + 1], recv_sem=grecv.at[3 * w + 1],
                    device_id=(ty * NZ + z, fk), device_id_type=MESH).start()

    def x_stage(w, yrec, xsel, wt):
        wait_for(yrec.at[pl.ds(0, NY - 1)], grecv.at[3 * w + 1])
        piece = yrec[0].astype(jnp.float32)
        for sy in range(1, NY):
            piece += yrec[sy].astype(jnp.float32)
        piece = piece.astype(jnp.bfloat16)
        xsel[...] = piece
        wt[:, x] = piece
        for dx in (2, 1, 3):
            tx = (x + dx) % NX
            pltpu.make_async_remote_copy(
                src_ref=xsel, dst_ref=wt.at[:, x],
                send_sem=gsend.at[3 * w + 2], recv_sem=grecv.at[3 * w + 2],
                device_id=(me, tx * NC + c), device_id_type=MESH).start()

    def x_wait(w, wt):
        wait_for(wt.at[:, pl.ds(0, NX - 1)], grecv.at[3 * w + 2])

    def chunk_out(o, wt, s_ref, r_ref):
        def product(tz):
            rows = tri[:, tz].reshape(NY * BS, SLOTS * BS)
            weights = wt[...].reshape(SLOTS * BS, CHUNK)
            half = jnp.dot(rows, weights, preferred_element_type=jnp.float32)
            s_ref[:, tz] = half.astype(jnp.bfloat16).reshape(NY, BS, CHUNK)

        def send(ty, tz):
            pltpu.make_async_remote_copy(
                src_ref=s_ref.at[ty, tz], dst_ref=r_ref.at[me],
                send_sem=asend.at[o], recv_sem=arecv.at[o],
                device_id=(ty * NZ + tz, fk), device_id_type=MESH).start()

        def step(q, carry):
            tz = far_first(q) if o == 2 else away(q)
            product(tz)
            for dy in range(NY):
                send((y + dy) % NY, tz)
            return carry

        lax.fori_loop(1, NZ, step, 0)
        product(z)
        for dy in range(1, NY):
            send((y + dy) % NY, z)
        r_ref[me] = s_ref[y, z]

    pair_lane = lax.broadcasted_iota(jnp.int32, (BS, 2 * BS), 1)

    def group(r_ref, tx, tc, store):
        base = (tx * NC + tc) * 16
        for j in range(8):
            lo, hi = base + j, base + 8 + j
            left = jnp.concatenate([r_ref[kept_ref[0, lo]], r_ref[kept_ref[0, hi]]], axis=0)
            right = jnp.concatenate([r_ref[kept_ref[1, lo]], r_ref[kept_ref[1, hi]]], axis=0)
            both = lax.dot_general(left, right, (((1,), (1,)), ((), ())), preferred_element_type=jnp.float32)
            store(j, jnp.where(pair_lane < BS, both[:BS], both[BS:]).reshape(NY, 16, 2 * BS))

    mine = z % 2 == c
    z_send_coef(0, g0, c, z)

    @pl.when(mine)
    def _():
        z_send_coef(1, g1, 2, z // 2)

    wait_for(g0.at[pl.ds(0, NZ - 1)], grecv.at[0])
    y_stage(0, g0, ysel0, yrec0)
    x_stage(0, yrec0, x0, w0)

    @pl.when(mine)
    def _():
        wait_for(g1.at[pl.ds(0, NZ // 2 - 1)], grecv.at[3])

    @pl.when(jnp.logical_not(mine))
    def _():
        wait_for(g1, grecv.at[3])

    y_stage(1, g1, ysel1, yrec1)
    load.wait()
    x_wait(0, w0)
    swap = pltpu.make_async_remote_copy(
        src_ref=w0, dst_ref=w1, send_sem=gsend.at[6], recv_sem=grecv.at[6],
        device_id=(me, sib), device_id_type=MESH)
    swap.start()
    chunk_out(0, w0, s0, r0)
    x_stage(1, yrec1, x1, w2)
    swap.wait()
    chunk_out(1, w1, s1, r1)
    x_wait(1, w2)
    merge = pltpu.make_async_remote_copy(
        src_ref=w2, dst_ref=w3, send_sem=gsend.at[7], recv_sem=grecv.at[7],
        device_id=(me, sib), device_id_type=MESH)
    merge.start()
    merge.wait()
    w2[...] = (w2[...].astype(jnp.float32) + w3[...].astype(jnp.float32)).astype(jnp.bfloat16)
    chunk_out(2, w2, s2, r2)

    for o, r_ref in ((0, r0), (1, r1)):
        wait_for(r_ref.at[pl.ds(0, NAUX_DEV - 1)], arecv.at[o])

        def all_groups(t, carry):
            tx, tc = t // NC, t % NC

            def store(j, pick):
                if o == 0:
                    kacc[tx, tc, j] = pick
                else:
                    kacc[tx, tc, j] += pick

            group(r_ref, tx, tc, store)
            return carry

        lax.fori_loop(0, NX * NC, all_groups, 0)

    def core_copy(tx):
        return pltpu.make_async_remote_copy(
            src_ref=kacc.at[tx, 1 - c], dst_ref=cb.at[tx],
            send_sem=csend.at[tx], recv_sem=crecv.at[tx],
            device_id=(me, sib), device_id_type=MESH)

    for dx in range(1, NX + 1):
        core_copy((x + dx) % NX).start()
    for dx in range(1, NX + 1):
        tx = (x + dx) % NX
        core_copy(tx).wait_recv()
        xs[tx] = kacc[tx, c] + cb[tx]
        if dx < NX:
            pltpu.make_async_remote_copy(
                src_ref=xs.at[tx], dst_ref=xb.at[x], send_sem=tsend.at[0], recv_sem=trecv.at[0],
                device_id=(me, tx * NC + c), device_id_type=MESH).start()

    wait_for(xb.at[pl.ds(0, NX - 1)], trecv.at[0])
    for dy in range(1, NY + 1):
        ty = (y + dy) % NY
        total = xs[x, :, ty]
        for dx in range(1, NX):
            total += xb[(x + dx) % NX, :, ty]
        ys[ty] = total
        if dy < NY:
            pltpu.make_async_remote_copy(
                src_ref=ys.at[ty], dst_ref=yb.at[y], send_sem=tsend.at[1], recv_sem=trecv.at[1],
                device_id=(ty * NZ + z, fk), device_id_type=MESH).start()

    wait_for(yb.at[pl.ds(0, NY - 1)], trecv.at[1])
    total = ys[y]
    for dy in range(1, NY):
        total += yb[(y + dy) % NY]
    early[...] = total
    for tx in range(NX):
        wait_for(cb.at[tx], csend.at[tx])

    wait_for(r2.at[pl.ds(0, NAUX_DEV - 1)], arecv.at[2])

    def core_copy2(tx):
        return pltpu.make_async_remote_copy(
            src_ref=kst.at[tx], dst_ref=cb2.at[tx],
            send_sem=c2send.at[tx], recv_sem=c2recv.at[tx],
            device_id=(me, sib), device_id_type=MESH)

    def theirs(tx):
        def store(j, pick):
            kst[tx, j] = pick.astype(jnp.bfloat16)

        group(r2, tx, 1 - c, store)
        core_copy2(tx).start()

    def ours(tx):
        def store(j, pick):
            kacc[tx, c, j] = pick

        group(r2, tx, c, store)
        core_copy2(tx).wait_recv()
        for half in range(2):
            pick = kacc[tx, c, half * 4:half * 4 + 4] + cb2[tx, half * 4:half * 4 + 4].astype(jnp.float32)
            pick = pick.astype(jnp.bfloat16)
            if half == 0:
                a1s[tx] = pick
            else:
                for ty in range(NY):
                    b1s[ty, tx] = pick[:, ty]

    def send_y(tx):
        for dy in (2, 1, 3):
            ty = (y + dy) % NY
            pltpu.make_async_remote_copy(
                src_ref=b1s.at[ty, tx], dst_ref=b1r.at[y, tx], send_sem=tsend.at[3], recv_sem=trecv.at[3],
                device_id=(ty * NZ + z, fk), device_id_type=MESH).start()

    def both_step(d, carry):
        theirs((x + NX - 1 - d) % NX)
        tx = (x + NX - d) % NX
        ours(tx)
        pltpu.make_async_remote_copy(
            src_ref=a1s.at[tx], dst_ref=a1r.at[x], send_sem=tsend.at[2], recv_sem=trecv.at[2],
            device_id=(me, tx * NC + c), device_id_type=MESH).start()
        send_y(tx)
        return carry

    theirs((x + NX - 1) % NX)
    lax.fori_loop(1, NX, both_step, 0)
    ours(x)
    send_y(x)

    wait_for(a1r.at[pl.ds(0, NX - 1)], trecv.at[2])
    for dy in (2, 1, 3, NY):
        ty = (y + dy) % NY
        total = a1s[x, :, ty].astype(jnp.float32)
        for dx in range(1, NX):
            total += a1r[(x + dx) % NX, :, ty].astype(jnp.float32)
        if dy < NY:
            a2s[ty] = total.astype(jnp.bfloat16)
            pltpu.make_async_remote_copy(
                src_ref=a2s.at[ty], dst_ref=a2r.at[y], send_sem=tsend.at[4], recv_sem=trecv.at[4],
                device_id=(ty * NZ + z, fk), device_id_type=MESH).start()
        else:
            vb[0:4] = total + early[0:4]

    wait_for(b1r.at[pl.ds(0, NY - 1)], trecv.at[3])
    for dx in (2, 1, 3, NX):
        tx = (x + dx) % NX
        total = b1s[y, tx].astype(jnp.float32)
        for dy in range(1, NY):
            total += b1r[(y + dy) % NY, tx].astype(jnp.float32)
        if dx < NX:
            b2s[tx] = total.astype(jnp.bfloat16)
            pltpu.make_async_remote_copy(
                src_ref=b2s.at[tx], dst_ref=b2r.at[x], send_sem=tsend.at[5], recv_sem=trecv.at[5],
                device_id=(me, tx * NC + c), device_id_type=MESH).start()
        else:
            vb[4:8] = total + early[4:8]

    wait_for(a2r.at[pl.ds(0, NY - 1)], trecv.at[4])
    total = vb[0:4]
    for dy in range(1, NY):
        total += a2r[(y + dy) % NY].astype(jnp.float32)
    vb[0:4] = total
    wait_for(b2r.at[pl.ds(0, NX - 1)], trecv.at[5])
    total = vb[4:8]
    for dx in range(1, NX):
        total += b2r[(x + dx) % NX].astype(jnp.float32)
    vb[4:8] = total
    for m in range(NZ):
        zs[m] = vb[:, m, :]

    def z_send(d, carry):
        tz = far_first(d)
        pltpu.make_async_remote_copy(
            src_ref=zs.at[tz], dst_ref=zb.at[z], send_sem=tsend.at[6], recv_sem=trecv.at[6],
            device_id=(y * NZ + tz, fk), device_id_type=MESH).start()
        return carry

    lax.fori_loop(1, NZ, z_send, 0)
    zb[z] = zs[z]
    wait_for(zb.at[pl.ds(0, NZ - 1)], trecv.at[6])
    result = jnp.sum(zb[...], axis=0)
    out_ref[0:8, :] = result[:, :BS]
    out_ref[8:16, :] = result[:, BS:]

    wait_for(g0.at[pl.ds(0, NZ - 1)], gsend.at[0])

    @pl.when(mine)
    def _():
        for rows in (NZ // 2, NZ // 2 - 1):
            wait_for(g1.at[pl.ds(0, rows)], gsend.at[3])

    for w, yrec, xsel in ((0, yrec0, x0), (1, yrec1, x1)):
        wait_for(yrec.at[pl.ds(0, NY - 1)], gsend.at[3 * w + 1])
        for _ in range(NX - 1):
            wait_for(xsel, gsend.at[3 * w + 2])
    for o, r_ref in ((0, r0), (1, r1), (2, r2)):
        wait_for(r_ref.at[pl.ds(0, NAUX_DEV - 1)], asend.at[o])
    for tx in range(NX):
        wait_for(cb2.at[tx], c2send.at[tx])
    wait_for(xb.at[pl.ds(0, NX - 1)], tsend.at[0])
    wait_for(yb.at[pl.ds(0, NY - 1)], tsend.at[1])
    wait_for(a1r.at[pl.ds(0, NX - 1)], tsend.at[2])
    wait_for(b1r.at[pl.ds(0, NY - 1)], tsend.at[3])
    wait_for(a2r.at[pl.ds(0, NY - 1)], tsend.at[4])
    wait_for(b2r.at[pl.ds(0, NX - 1)], tsend.at[5])
    wait_for(zb.at[pl.ds(0, NZ - 1)], tsend.at[6])


def per_device(three_index, col_blocks, pair_mask, occ_coef, occ_mask, kept):
    fock_count = lax.axis_size("fock")
    naux, rows, width = three_index.shape
    factor = float(naux * fock_count * occ_coef.shape[1]) ** (-0.5)
    bf, f32 = jnp.bfloat16, jnp.float32
    vmem = pl.BlockSpec(memory_space=pltpu.VMEM)
    dma = pltpu.SemaphoreType.DMA
    g = pltpu.VMEM((NZ, 16, CHUNK), bf)
    ysel = pltpu.VMEM((NY, SLOTS, 16, CHUNK), bf)
    xsel = pltpu.VMEM((SLOTS, 16, CHUNK), bf)
    wt = pltpu.VMEM((SLOTS, NX, 16, CHUNK), bf)
    send = pltpu.VMEM((NY, NZ, BS, CHUNK), bf)
    recv = pltpu.VMEM((NAUX_DEV, BS, CHUNK), bf)
    first = pltpu.VMEM((4, 4, 4, 16, 2 * BS), bf)
    second = pltpu.VMEM((4, 4, 16, 2 * BS), bf)
    total = pl.pallas_call(
        kernel,
        out_shape=jax.ShapeDtypeStruct((16, BS), f32),
        in_specs=[pl.BlockSpec(memory_space=pl.ANY)] * 6,
        out_specs=vmem,
        scratch_shapes=[
            pltpu.SMEM((SLOTS, NAUX_DEV), jnp.int32),
            pltpu.SMEM((SLOTS, NAUX_DEV), jnp.int32),
            pltpu.VMEM(occ_coef.shape, bf),
            pltpu.SMEM((2 * CHUNKS, NAUX_DEV), jnp.int32),
            pltpu.SMEM((2, kept.shape[0]), jnp.int32),
            dma((5,)),
            pltpu.VMEM((NY, NZ, rows, width), bf),
            pltpu.VMEM((CHUNKS, NX, 16, CHUNK), bf),
            g, pltpu.VMEM((NZ // 2, 16, CHUNK), bf), ysel, ysel, ysel, ysel, xsel, xsel, wt, wt, wt, wt, send, send, send, recv, recv, recv,
            pltpu.VMEM((NX, NC, 8, NY, 16, 2 * BS), f32),
            pltpu.VMEM((NX, 8, NY, 16, 2 * BS), f32),
            pltpu.VMEM((NX, 8, NY, 16, 2 * BS), f32),
            pltpu.VMEM((NX, 8, NY, 16, 2 * BS), f32),
            pltpu.VMEM((NY, 8, 16, 2 * BS), f32),
            pltpu.VMEM((NY, 8, 16, 2 * BS), f32),
            pltpu.VMEM((8, 16, 2 * BS), f32),
            pltpu.VMEM((NX, 8, NY, 16, 2 * BS), bf),
            pltpu.VMEM((NX, 8, NY, 16, 2 * BS), bf),
            first, first, first, first, second, second, second, second,
            pltpu.VMEM((8, 16, 2 * BS), f32),
            pltpu.VMEM((NZ, 8, 2 * BS), f32),
            pltpu.VMEM((NZ, 8, 2 * BS), f32),
            dma, dma((8,)), dma((8,)), dma((3,)), dma((3,)), dma((4,)), dma((4,)), dma((4,)), dma((4,)),
            dma((7,)), dma((7,)),
        ],
        compiler_params=pltpu.CompilerParams(
            collective_id=0, has_side_effects=True, vmem_limit_bytes=62 * 2**20),
        cost_estimate=pl.CostEstimate(flops=2_400_000_000, bytes_accessed=8_000_000, transcendentals=0),
    )(three_index.reshape(NY, NZ, rows, width), col_blocks.T, pair_mask.T, occ_coef, occ_mask.T, kept.T)
    return total * factor


def solution(mesh):
    in_specs = (P("fock", "aux", None), P(), P(), P("aux", None), P(), P())
    out_specs = P("fock", "aux")
    return jax.shard_map(
        per_device, mesh=mesh, in_specs=in_specs, out_specs=out_specs, check_vma=False
    )
```
